32 devices in a mesh: group: 2 (over core), dp: 8 (over z, x), mp: 2 (over y).
Axes of the slice: x: 2, y: 2, z: 4, core: 2. Of those that a mesh axis runs over, the one named last changes fastest.
Arguments:
- noise_seeds: int32 [16], P(('group', 'dp')), may hold values from 0 to 16777215
- timestep_ids: int32 [16], P(('group', 'dp')), may hold values from 0 to 999
- gen_up: bfloat16 [3072, 6144], P(('group', 'dp'), 'mp'), may hold values from -0.109375 to 0.109375
- gen_down: bfloat16 [6144, 3072], P('mp', ('group', 'dp')), may hold values from -0.08930431 to 0.08930431
- score_qkv: bfloat16 [2, 3, 3072, 3072], P('group', None, None, 'mp'), may hold values from -0.109375 to 0.109375
- score_out: bfloat16 [2, 3072, 3072], P('group', 'mp'), may hold values from -0.109375 to 0.109375
Outputs:
- latents: bfloat16 [16, 256, 3072], P(('group', 'dp'), None, 'mp')
- score_gap: bfloat16 [16, 256, 3072], P(('group', 'dp'), None, 'mp')
- grad_up: bfloat16 [3072, 6144], P(('group', 'dp'), 'mp')
- grad_down: bfloat16 [6144, 3072], P('mp', ('group', 'dp'))
The draws below stay inside these ranges and needn't reach their ends.
All inputs are finite; a program needn't handle non-finite values.
Results may differ from the reference program's by a relative error of at most 0.03.
Values may be sent and summed in bfloat16 or wider, within the bound.
A program may use at most 192 MiB of HBM per device.

```python
import jax
import jax.numpy as jnp
from jax import lax

D = 3072
HEADS = 24
HEAD_DIM = 128
FF = 6144
SEQ = 256
STEPS = 1000
BATCH = 16
N_MP = 2


def draw_gen_down(key, part):
    scale = FF ** (-0.5)
    base = jnp.clip(jax.random.normal(key, (FF, D), jnp.float32), -6.0, 6.0)
    centred = base - jnp.mean(base, axis=0, keepdims=True)
    return (centred * scale).astype(jnp.bfloat16)


def place_ends(result, stream_key, low, largest):
    place = [jax.random.randint(jax.random.fold_in(stream_key, axis), (), 0, length) for axis, length in enumerate(result.shape)]
    longest = result.shape.index(max(result.shape))
    neighbour = place[:longest] + [(place[longest] + 1) % result.shape[longest]] + place[longest + 1:]
    return result.at[tuple(place)].set(low).at[tuple(neighbour)].set(largest)


def levels(rng, shape, pieces, low, high):
    level, own = 1.0, jax.random.fold_in(rng, 6)
    for axis_at, shards_of in pieces:
        steps = jnp.exp(jax.random.uniform(jax.random.fold_in(own, axis_at), (shards_of,), jnp.float32, low / len(pieces), high / len(pieces)))
        level = level * jnp.repeat(steps, shape[axis_at] // shards_of).reshape([-1 if axis == axis_at else 1 for axis in range(len(shape))])
    return level


def bell_draw(key, shape, deviation, most, pieces=(), kind=jnp.bfloat16):
    array = deviation * jax.random.normal(key, shape, jnp.float32)
    if pieces:
        array = array * levels(key, shape, pieces, -0.22, 0.18)
    return jnp.clip(array, -most, most).astype(kind)


def setup_inputs(seed: int = 0) -> dict:
    arg_keys = jax.random.split(jax.random.key(seed), 7)
    noise_seeds = place_ends(jax.random.randint(arg_keys[0], (BATCH,), 0, 16777216), jax.random.fold_in(arg_keys[0], 1), 0, 16777215).astype(jnp.int32)
    timestep_ids = place_ends(jax.random.randint(arg_keys[1], (BATCH,), 0, STEPS), jax.random.fold_in(arg_keys[1], 1), 0, STEPS - 1).astype(jnp.int32)
    gen_up = bell_draw(arg_keys[2], (D, FF), D ** -0.5, 0.109375, ((0, 16), (1, 2)))
    gen_down = draw_gen_down(jax.random.fold_in(arg_keys[6], 71), 0)
    score_qkv = bell_draw(arg_keys[4], (2, 3, D, D), D ** -0.5, 0.109375, ((0, 2), (3, 2)))
    score_out = bell_draw(arg_keys[5], (2, D, D), D ** -0.5, 0.109375, ((0, 2), (1, 2)))
    return dict(noise_seeds=noise_seeds, timestep_ids=timestep_ids, gen_up=gen_up, gen_down=gen_down, score_qkv=score_qkv, score_out=score_out)


NORM_EPS = 1e-06
ROOT_THREE = 1.7320508
GELU_SCALE = 0.7978845608

def hashed(seed_grid, stream, feat_start, feat_count, length):
    shape = (1, length, feat_count)
    tokens = lax.broadcasted_iota(jnp.int32, shape, 1)
    feature = lax.broadcasted_iota(jnp.int32, shape, 2) + feat_start
    mixing = seed_grid * 747796405 + stream * 374761393 + tokens * 1103515245 + feature * 668265263
    mixing = mixing ^ mixing >> 15
    mixing = mixing * 1274126177
    mixing = mixing ^ mixing >> 13
    mixing = mixing * 1911520717
    mixing = mixing ^ mixing >> 16
    level = (mixing >> 7 & 65535).astype(jnp.float32)
    return ((level + 0.5) * (2.0 / 65536.0) - 1.0) * ROOT_THREE

def rms_norm(value):
    return value * lax.rsqrt(lax.optimization_barrier(jnp.mean(value * value, axis=-1, keepdims=True)) + NORM_EPS)

def gelu_slope(value):
    inner = GELU_SCALE * (value + 0.044715 * value * value * value)
    bend = jnp.tanh(inner)
    return 0.5 * (1.0 + bend) + 0.5 * value * (1.0 - bend * bend) * GELU_SCALE * (1.0 + 3.0 * 0.044715 * value * value)

def rounded(value):
    return lax.optimization_barrier(value.astype(jnp.bfloat16)).astype(jnp.float32)

def block_sum(left, right, blocks):
    size = left.shape[1] // blocks
    total = jnp.zeros((left.shape[0], right.shape[1]), jnp.float32)
    for block in range(blocks):
        term = jnp.dot(left[:, block * size:(block + 1) * size], right[block * size:(block + 1) * size], preferred_element_type=jnp.float32)
        total = total + rounded(term)
    return total

def score_net(noisy, weights_in, weights_out):
    normed = rms_norm(noisy.astype(jnp.float32)).astype(jnp.bfloat16).reshape(BATCH * SEQ, D)
    shape = (BATCH, SEQ, HEADS, HEAD_DIM)
    query = jnp.dot(normed, weights_in[0], preferred_element_type=jnp.float32).astype(jnp.bfloat16).reshape(shape)
    keys = jnp.dot(normed, weights_in[1], preferred_element_type=jnp.float32).astype(jnp.bfloat16).reshape(shape)
    values = jnp.dot(normed, weights_in[2], preferred_element_type=jnp.float32).astype(jnp.bfloat16).reshape(shape)

    def attend(triple):
        asked, keyed, valued = triple
        scores = jnp.einsum('qhe,khe->hqk', asked.astype(jnp.float32), keyed.astype(jnp.float32)) * HEAD_DIM ** (-0.5)
        expo = jnp.exp(scores)
        probs = (expo / lax.optimization_barrier(jnp.sum(expo, axis=-1, keepdims=True))).astype(jnp.bfloat16)
        return jnp.einsum('hqk,khe->qhe', probs.astype(jnp.float32), valued.astype(jnp.float32)).astype(jnp.bfloat16)
    attended = lax.map(attend, (query, keys, values)).reshape(BATCH * SEQ, D)
    return block_sum(attended, weights_out, N_MP).astype(jnp.bfloat16).reshape(BATCH, SEQ, D)

def reference(noise_seeds, timestep_ids, gen_up, gen_down, score_qkv, score_out):
    seed_grid = noise_seeds[:, None, None]
    start_noise = hashed(seed_grid, 0, 0, D, SEQ)
    normed = rms_norm(start_noise).astype(jnp.bfloat16).reshape(BATCH * SEQ, D)
    before = jnp.dot(normed, gen_up, preferred_element_type=jnp.float32)
    hidden = jax.nn.gelu(before, approximate=True).astype(jnp.bfloat16)
    mixed = block_sum(hidden, gen_down, N_MP)
    latents = (start_noise + mixed.reshape(BATCH, SEQ, D)).astype(jnp.bfloat16)
    shift = ((timestep_ids.astype(jnp.float32) + 0.5) / STEPS)[:, None, None]
    fresh = hashed(seed_grid, 1, 0, D, SEQ)
    noisy = ((1.0 - shift) * latents.astype(jnp.float32) + shift * fresh).astype(jnp.bfloat16)
    real_pred = score_net(noisy, score_qkv[0], score_out[0])
    fake_pred = score_net(noisy, score_qkv[1], score_out[1])
    score_gap = (fake_pred.astype(jnp.float32) - real_pred.astype(jnp.float32)).astype(jnp.bfloat16)

    def accumulate(carry, items):
        grad_u, grad_d = carry
        hid, nrm, bef, gapped = items
        down_term = jnp.dot(hid.T, gapped, preferred_element_type=jnp.float32) / BATCH
        slope = jnp.dot(gapped, gen_down.T, preferred_element_type=jnp.float32)
        change = (slope * gelu_slope(bef)).astype(jnp.bfloat16)
        up_term = jnp.dot(nrm.T, change, preferred_element_type=jnp.float32) / BATCH
        return ((grad_u + rounded(up_term), grad_d + rounded(down_term)), None)
    start = (jnp.zeros((D, FF), jnp.float32), jnp.zeros((FF, D), jnp.float32))
    items = (hidden.reshape(BATCH, SEQ, FF), normed.reshape(BATCH, SEQ, D), before.reshape(BATCH, SEQ, FF), score_gap)
    (grad_u, grad_d), unused = lax.scan(accumulate, start, items)
    return (latents, score_gap, grad_u.astype(jnp.bfloat16), grad_d.astype(jnp.bfloat16))
```

```python
import jax
import jax.numpy as jnp
from jax import lax
from jax.sharding import PartitionSpec as P

D = 3072
HEAD_DIM = 128
SEQ = 256
STEPS = 1000


NORM_EPS = 1e-06
ROOT_THREE = 1.7320508
GELU_SCALE = 0.7978845608


def swap(shard, axis, bit):
    return lax.ppermute(shard, axis, [(i, i ^ bit) for i in range(lax.axis_size(axis))])


def bits_of(axis):
    return [1 << k for k in range(lax.axis_size(axis).bit_length() - 1)]


def xor_gather(shard, axis, order):
    bits = bits_of(axis)
    out = shard.reshape((1,) * len(bits) + shard.shape)
    for bit in order:
        out = jnp.concatenate([out, swap(out, axis, bit)], axis=bits.index(bit))
    return out


def xor_scatter(parts, axis, order):
    bits = bits_of(axis)
    for bit in order:
        at = bits.index(bit)
        kept = lax.slice_in_dim(parts, 0, 1, axis=at)
        sent = lax.slice_in_dim(parts, 1, 2, axis=at).astype(jnp.bfloat16)
        parts = kept.astype(jnp.float32) + swap(sent, axis, bit).astype(jnp.float32)
    return parts.reshape(parts.shape[len(bits):])


def tokens_to_features(shard, axis):
    count = lax.axis_size(axis)
    me = lax.axis_index(axis)
    tokens, width = shard.shape[0], shard.shape[1] // count
    out = jnp.zeros((count * tokens, width), shard.dtype)
    for mask in range(count):
        other = me ^ mask
        block = lax.dynamic_slice_in_dim(shard, other * width, width, 1)
        if mask:
            block = swap(block, axis, mask)
        out = lax.dynamic_update_slice_in_dim(out, block, other * tokens, 0)
    return out


def hashed(seed_grid, stream, tokens, feature):
    mixing = seed_grid * 747796405 + stream * 374761393 + tokens * 1103515245 + feature * 668265263
    mixing = mixing ^ mixing >> 15
    mixing = mixing * 1274126177
    mixing = mixing ^ mixing >> 13
    mixing = mixing * 1911520717
    mixing = mixing ^ mixing >> 16
    level = (mixing >> 7 & 65535).astype(jnp.float32)
    return ((level + 0.5) * (2.0 / 65536.0) - 1.0) * ROOT_THREE


def rms_norm(value):
    return value * lax.rsqrt(jnp.mean(value * value, axis=-1, keepdims=True) + NORM_EPS)


def gelu_slope(value):
    inner = GELU_SCALE * (value + 0.044715 * value * value * value)
    bend = jnp.tanh(inner)
    return 0.5 * (1.0 + bend) + 0.5 * value * (1.0 - bend * bend) * GELU_SCALE * (
        1.0 + 3.0 * 0.044715 * value * value
    )


def score_forward(normed, weights_in, weights_out):
    pairs, length = normed.shape[:2]
    local_heads = weights_in.shape[2] // HEAD_DIM
    projected = jnp.einsum(
        "bsd,kdh->kbsh", normed, weights_in, preferred_element_type=jnp.float32
    ).astype(jnp.bfloat16)
    shape = (pairs, length, local_heads, HEAD_DIM)
    query = projected[0].reshape(shape)
    keys = projected[1].reshape(shape)
    values = projected[2].reshape(shape)
    scores = jnp.einsum(
        "bqhe,bkhe->bhqk", query, keys, preferred_element_type=jnp.float32
    ) * HEAD_DIM ** (-0.5)
    expo = jnp.exp(scores)
    probs = (expo / jnp.sum(expo, axis=-1, keepdims=True)).astype(jnp.bfloat16)
    attended = jnp.einsum(
        "bhqk,bkhe->bqhe", probs, values, preferred_element_type=jnp.float32
    ).astype(jnp.bfloat16)
    attended = attended.reshape(pairs, length, local_heads * HEAD_DIM)
    return [
        jnp.dot(attended[pair], weights_out, preferred_element_type=jnp.float32)
        for pair in (1, 0)
    ]


def contract_first(left, right):
    return lax.dot_general(left, right, (((0,), (0,)), ((), ())), preferred_element_type=jnp.float32)


def per_device(noise_seeds, timestep_ids, gen_up, gen_down, score_qkv, score_out):
    n_dp, n_mp = lax.axis_size("dp"), lax.axis_size("mp")
    batch_size = lax.axis_size("group") * n_dp
    group, mp = lax.axis_index("group"), lax.axis_index("mp")
    dp_bits, mp_bits = bits_of("dp"), bits_of("mp")
    near_first = dp_bits
    far_first = dp_bits[1:] + dp_bits[:1]
    length = SEQ // n_mp
    half = D // 2

    up = lax.all_to_all(gen_up, "dp", split_axis=1, concat_axis=0, tiled=True)
    down = lax.all_to_all(gen_down, "dp", split_axis=0, concat_axis=1, tiled=True)
    share = up.shape[1]
    up = xor_gather(up, "mp", mp_bits).reshape(n_mp, half, share)
    up = up.transpose(1, 0, 2).reshape(half, n_mp * share)
    up = jnp.concatenate([up, swap(up, "group", 1)], axis=0)
    down = xor_gather(down, "mp", mp_bits).reshape(n_mp * share, half)
    down_other = swap(down, "group", 1)
    down = jnp.where(
        group == 0,
        jnp.concatenate([down, down_other], axis=1),
        jnp.concatenate([down_other, down], axis=1),
    )

    seeds = xor_gather(noise_seeds, "dp", near_first).reshape(n_dp, 1, 1)
    shape = (n_dp, length, D)
    tokens = lax.broadcasted_iota(jnp.int32, shape, 1) + mp * length
    feature = (lax.broadcasted_iota(jnp.int32, shape, 2) + group * half) % D
    normed = rms_norm(hashed(seeds, 0, tokens, feature)).astype(jnp.bfloat16)
    normed = normed.reshape(n_dp * length, D)
    before = jnp.dot(normed, up, preferred_element_type=jnp.float32)
    hidden = jax.nn.gelu(before, approximate=True).astype(jnp.bfloat16)

    def stacked(value):
        return value.reshape((2,) * len(dp_bits) + (length, value.shape[-1]))

    cut = D * 2 // 3
    near = jnp.dot(hidden, down[:, :cut], preferred_element_type=jnp.float32).astype(jnp.bfloat16)
    far = jnp.dot(hidden, down[:, cut:], preferred_element_type=jnp.float32).astype(jnp.bfloat16)
    mixed = jnp.concatenate(
        [
            xor_scatter(stacked(near), "dp", near_first),
            xor_scatter(stacked(far), "dp", far_first),
        ],
        axis=-1,
    )

    own_seed = noise_seeds[:, None]
    tokens = lax.broadcasted_iota(jnp.int32, (length, D), 0) + mp * length
    feature = lax.broadcasted_iota(jnp.int32, (length, D), 1)
    latent = (hashed(own_seed, 0, tokens, feature) + mixed).astype(jnp.bfloat16)
    shift = (timestep_ids.astype(jnp.float32) + 0.5) / STEPS
    fresh = hashed(own_seed, 1, tokens, feature)
    noisy = ((1.0 - shift) * latent.astype(jnp.float32) + shift * fresh).astype(jnp.bfloat16)
    score_normed = rms_norm(noisy.astype(jnp.float32)).astype(jnp.bfloat16)

    sample = xor_gather(score_normed, "mp", mp_bits).reshape(SEQ, D)
    paired = jnp.stack([sample, swap(sample, "group", 1)])
    latents = tokens_to_features(latent, "mp")
    other_pred, own_pred = score_forward(paired, score_qkv[0], score_out[0])
    partner = swap(other_pred.astype(jnp.bfloat16), "group", 1)
    flip_sign = (2 * group - 1).astype(jnp.float32)
    gap = flip_sign * (own_pred - partner.astype(jnp.float32))
    gap = xor_scatter(gap.reshape((2,) * len(mp_bits) + (length, D)), "mp", mp_bits)
    gap = gap.astype(jnp.bfloat16)
    gap_all = jnp.concatenate(
        [
            xor_gather(gap[:, :cut], "dp", near_first[::-1]).reshape(n_dp * length, cut),
            xor_gather(gap[:, cut:], "dp", far_first[::-1]).reshape(n_dp * length, D - cut),
        ],
        axis=1,
    )
    score_gap = tokens_to_features(gap, "mp")

    def over_batch(value):
        return value / batch_size

    down_sent = over_batch(
        contract_first(hidden, lax.dynamic_slice_in_dim(gap_all, (1 - group) * half, half, 1))
    ).astype(jnp.bfloat16)
    down_sent = swap(down_sent, "group", 1)
    down_kept = over_batch(
        contract_first(hidden, lax.dynamic_slice_in_dim(gap_all, group * half, half, 1))
    )
    grad_down = (down_kept + down_sent.astype(jnp.float32)).astype(jnp.bfloat16)
    grad_down = grad_down.reshape((2,) * len(mp_bits) + (share, half))
    grad_down = xor_scatter(grad_down, "mp", mp_bits).astype(jnp.bfloat16)
    grad_down = lax.all_to_all(grad_down, "dp", split_axis=1, concat_axis=0, tiled=True)

    slope = lax.dot_general(
        gap_all, down, (((1,), (1,)), ((), ())), preferred_element_type=jnp.float32
    )
    change = (slope * gelu_slope(before)).astype(jnp.bfloat16)
    up_sent = over_batch(contract_first(normed[:, half:], change)).astype(jnp.bfloat16)
    up_sent = swap(up_sent, "group", 1)
    up_kept = over_batch(contract_first(normed[:, :half], change))
    grad_up = (up_kept + up_sent.astype(jnp.float32)).astype(jnp.bfloat16)
    grad_up = jnp.moveaxis(grad_up.reshape(half, n_mp, share), 1, 0)
    grad_up = grad_up.reshape((2,) * len(mp_bits) + (half, share))
    grad_up = xor_scatter(grad_up, "mp", mp_bits).astype(jnp.bfloat16)
    grad_up = lax.all_to_all(grad_up, "dp", split_axis=0, concat_axis=1, tiled=True)
    return (latents[None], score_gap[None], grad_up, grad_down)


def solution(mesh):
    in_specs = (
        P(("group", "dp")),
        P(("group", "dp")),
        P(("group", "dp"), "mp"),
        P("mp", ("group", "dp")),
        P("group", None, None, "mp"),
        P("group", "mp", None),
    )
    out_specs = (
        P(("group", "dp"), None, "mp"),
        P(("group", "dp"), None, "mp"),
        P(("group", "dp"), "mp"),
        P("mp", ("group", "dp")),
    )
    return jax.shard_map(
        per_device, mesh=mesh, in_specs=in_specs, out_specs=out_specs, check_vma=False
    )
```

```python
import functools

import jax
import jax.numpy as jnp
from jax import lax
from jax.experimental import pallas as pl
from jax.experimental.pallas import tpu as pltpu
from jax.sharding import PartitionSpec as P

D = 3072
HEAD_DIM = 128
SEQ = 256
STEPS = 1000


NORM_EPS = 1e-06
ROOT_THREE = 1.7320508
GELU_SCALE = 0.7978845608


def swap(shard, axis, bit):
    return lax.ppermute(shard, axis, [(i, i ^ bit) for i in range(lax.axis_size(axis))])


def bits_of(axis):
    return [1 << k for k in range(lax.axis_size(axis).bit_length() - 1)]


def xor_gather(shard, axis, order):
    bits = bits_of(axis)
    out = shard.reshape((1,) * len(bits) + shard.shape)
    for bit in order:
        out = jnp.concatenate([out, swap(out, axis, bit)], axis=bits.index(bit))
    return out


def xor_scatter(parts, axis, order):
    bits = bits_of(axis)
    for bit in order:
        at = bits.index(bit)
        kept = lax.slice_in_dim(parts, 0, 1, axis=at)
        sent = lax.slice_in_dim(parts, 1, 2, axis=at).astype(jnp.bfloat16)
        parts = kept.astype(jnp.float32) + swap(sent, axis, bit).astype(jnp.float32)
    return parts.reshape(parts.shape[len(bits):])


def tokens_to_features(shard, axis):
    count = lax.axis_size(axis)
    me = lax.axis_index(axis)
    tokens, width = shard.shape[0], shard.shape[1] // count
    out = jnp.zeros((count * tokens, width), shard.dtype)
    for mask in range(count):
        other = me ^ mask
        block = lax.dynamic_slice_in_dim(shard, other * width, width, 1)
        if mask:
            block = swap(block, axis, mask)
        out = lax.dynamic_update_slice_in_dim(out, block, other * tokens, 0)
    return out


def hashed(seed_grid, stream, tokens, feature):
    mixing = seed_grid * 747796405 + stream * 374761393 + tokens * 1103515245 + feature * 668265263
    mixing = mixing ^ mixing >> 15
    mixing = mixing * 1274126177
    mixing = mixing ^ mixing >> 13
    mixing = mixing * 1911520717
    mixing = mixing ^ mixing >> 16
    level = (mixing >> 7 & 65535).astype(jnp.float32)
    return ((level + 0.5) * (2.0 / 65536.0) - 1.0) * ROOT_THREE


ROWS = 16


def greet(spot, line, pair):
    barrier = pltpu.get_barrier_semaphore()

    def signal(to):
        pl.semaphore_signal(
            barrier, inc=1, device_id={"dp": to}, device_id_type=pl.DeviceIdType.MESH
        )

    me = lax.axis_index("dp")
    signal(pair)

    @pl.when(spot > 0)
    def _():
        signal(me - 2)

    @pl.when(spot < line - 1)
    def _():
        signal(me + 2)

    ends = (spot == 0).astype(jnp.int32) + (spot == line - 1).astype(jnp.int32)
    pl.semaphore_wait(barrier, 3 - ends)


def remote(source, target, send_sem, recv_sem, to):
    return pltpu.make_async_remote_copy(
        src_ref=source,
        dst_ref=target,
        send_sem=send_sem,
        recv_sem=recv_sem,
        device_id={"dp": to},
        device_id_type=pl.DeviceIdType.MESH,
    )


def sum_kernel(line, parts, out, paired, lower, upper, p_send, p_recv, l_send, l_recv, u_send, u_recv):
    me = lax.axis_index("dp")
    side, spot = lax.rem(me, 2), lax.div(me, 2)
    pair = me + 1 - 2 * side
    steps = parts.shape[1] // ROWS
    greet(spot, line, pair)

    def to_pair(d):
        return remote(parts.at[2 * d + 1 - side], paired.at[d], p_send.at[d], p_recv.at[d], pair)

    def to_next(d):
        return remote(paired.at[d], lower.at[d], l_send.at[d], l_recv.at[d], me + 2)

    def to_last(d):
        return remote(paired.at[d], upper.at[d], u_send.at[d], u_recv.at[d], me - 2)

    def add(target, d, terms):
        @pl.loop(0, steps)
        def _(step):
            rows = pl.ds(pl.multiple_of(step * ROWS, ROWS), ROWS)
            total = parts[2 * d + side, rows].astype(jnp.float32)
            for term in terms:
                total = total + term[d, rows].astype(jnp.float32)
            if target is out:
                out[rows] = total
            else:
                target[d, rows] = total.astype(jnp.bfloat16)

    for far in range(line - 1, 0, -1):

        @pl.when(spot + far < line)
        def _():
            to_pair(spot + far).start()

        @pl.when(spot - far >= 0)
        def _():
            to_pair(spot - far).start()

    to_pair(spot).start()

    for far in range(line - 1, 0, -1):
        up, down = spot + far, spot - far

        @pl.when(up < line)
        def _():
            to_pair(up).wait_recv()

            @pl.when(spot > 0)
            def _():
                to_next(up).wait_recv()
                add(paired, up, (paired, lower))

            @pl.when(spot == 0)
            def _():
                add(paired, up, (paired,))

            to_next(up).start()

        @pl.when(down >= 0)
        def _():
            to_pair(down).wait_recv()

            @pl.when(spot < line - 1)
            def _():
                to_last(down).wait_recv()
                add(paired, down, (paired, upper))

            @pl.when(spot == line - 1)
            def _():
                add(paired, down, (paired,))

            to_last(down).start()

    to_pair(spot).wait_recv()

    @pl.when(spot == 0)
    def _():
        to_last(spot).wait_recv()
        add(out, spot, (paired, upper))

    @pl.when(spot == line - 1)
    def _():
        to_next(spot).wait_recv()
        add(out, spot, (paired, lower))

    @pl.when((spot > 0) & (spot < line - 1))
    def _():
        to_next(spot).wait_recv()
        to_last(spot).wait_recv()
        add(out, spot, (paired, lower, upper))

    for d in range(line):
        to_pair(d).wait_send()

        @pl.when(d > spot)
        def _():
            to_next(d).wait_send()

        @pl.when(d < spot)
        def _():
            to_last(d).wait_send()


def sum_over_dp(parts):
    line = parts.shape[0] // 2
    block = parts.shape[1:]
    slots = pltpu.VMEM((line,) + block, jnp.bfloat16)
    return pl.pallas_call(
        functools.partial(sum_kernel, line),
        out_shape=jax.ShapeDtypeStruct(block, jnp.float32),
        in_specs=[pl.BlockSpec(memory_space=pltpu.VMEM)],
        out_specs=pl.BlockSpec(memory_space=pltpu.VMEM),
        scratch_shapes=[slots] * 3 + [pltpu.SemaphoreType.DMA((line,))] * 6,
        compiler_params=pltpu.CompilerParams(
            collective_id=0, has_side_effects=True, vmem_limit_bytes=40 << 20
        ),
        cost_estimate=pl.CostEstimate(
            flops=2 * parts.size, bytes_accessed=40 * parts.size, transcendentals=0
        ),
    )(parts)


def gather_kernel(line, own, out, own_sem, recv, p_send, n_send, l_send):
    me = lax.axis_index("dp")
    side, spot = lax.rem(me, 2), lax.div(me, 2)
    pair = me + 1 - 2 * side
    greet(spot, line, pair)

    def source(d, first):
        return own if first else out.at[2 * d + side]

    def move(d, sems, to, first=False):
        b = 2 * d + side
        return remote(source(d, first), out.at[b], sems.at[d], recv.at[b], to)

    def arrived(b):
        remote(out.at[b], out.at[b], p_send.at[0], recv.at[b], pair).wait_recv()

    kept = pltpu.make_async_copy(own, out.at[me], own_sem)

    @pl.when(spot < line - 1)
    def _():
        move(spot, n_send, me + 2, True).start()

    @pl.when(spot > 0)
    def _():
        move(spot, l_send, me - 2, True).start()

    move(spot, p_send, pair, True).start()
    kept.start()
    for far in range(1, line):
        low, high = spot - far, spot + far

        @pl.when(low >= 0)
        def _():
            arrived(2 * low + side)

            @pl.when(spot < line - 1)
            def _():
                move(low, n_send, me + 2).start()

            move(low, p_send, pair).start()

        @pl.when(high < line)
        def _():
            arrived(2 * high + side)

            @pl.when(spot > 0)
            def _():
                move(high, l_send, me - 2).start()

            move(high, p_send, pair).start()

    for d in range(line):
        arrived(2 * d + 1 - side)
        move(d, p_send, pair).wait_send()

        @pl.when((d <= spot) & (spot < line - 1))
        def _():
            move(d, n_send, me + 2).wait_send()

        @pl.when((d >= spot) & (spot > 0))
        def _():
            move(d, l_send, me - 2).wait_send()

    kept.wait()


def gather_over_dp(own):
    count = lax.axis_size("dp")
    line = count // 2
    return pl.pallas_call(
        functools.partial(gather_kernel, line),
        out_shape=jax.ShapeDtypeStruct((count,) + own.shape, own.dtype),
        in_specs=[pl.BlockSpec(memory_space=pl.ANY)],
        out_specs=pl.BlockSpec(memory_space=pl.ANY),
        scratch_shapes=[
            pltpu.SemaphoreType.DMA(()),
            pltpu.SemaphoreType.DMA((count,)),
            pltpu.SemaphoreType.DMA((line,)),
            pltpu.SemaphoreType.DMA((line,)),
            pltpu.SemaphoreType.DMA((line,)),
        ],
        compiler_params=pltpu.CompilerParams(collective_id=1, has_side_effects=True),
        cost_estimate=pl.CostEstimate(
            flops=0, bytes_accessed=40 * count * own.size, transcendentals=0
        ),
    )(own)


def rms_norm(value):
    return value * lax.rsqrt(jnp.mean(value * value, axis=-1, keepdims=True) + NORM_EPS)


def gelu_slope(value):
    inner = GELU_SCALE * (value + 0.044715 * value * value * value)
    bend = jnp.tanh(inner)
    return 0.5 * (1.0 + bend) + 0.5 * value * (1.0 - bend * bend) * GELU_SCALE * (
        1.0 + 3.0 * 0.044715 * value * value
    )


def score_forward(normed, weights_in, weights_out):
    pairs, length = normed.shape[:2]
    local_heads = weights_in.shape[2] // HEAD_DIM
    projected = jnp.einsum(
        "bsd,kdh->kbsh", normed, weights_in, preferred_element_type=jnp.float32
    ).astype(jnp.bfloat16)
    shape = (pairs, length, local_heads, HEAD_DIM)
    query = projected[0].reshape(shape)
    keys = projected[1].reshape(shape)
    values = projected[2].reshape(shape)
    scores = jnp.einsum(
        "bqhe,bkhe->bhqk", query, keys, preferred_element_type=jnp.float32
    ) * HEAD_DIM ** (-0.5)
    expo = jnp.exp(scores)
    probs = (expo / jnp.sum(expo, axis=-1, keepdims=True)).astype(jnp.bfloat16)
    attended = jnp.einsum(
        "bhqk,bkhe->bqhe", probs, values, preferred_element_type=jnp.float32
    ).astype(jnp.bfloat16)
    attended = attended.reshape(pairs, length, local_heads * HEAD_DIM)
    return [
        jnp.dot(attended[pair], weights_out, preferred_element_type=jnp.float32)
        for pair in (1, 0)
    ]


def contract_first(left, right):
    return lax.dot_general(left, right, (((0,), (0,)), ((), ())), preferred_element_type=jnp.float32)


def per_device(noise_seeds, timestep_ids, gen_up, gen_down, score_qkv, score_out):
    n_dp, n_mp = lax.axis_size("dp"), lax.axis_size("mp")
    batch_size = lax.axis_size("group") * n_dp
    group, mp = lax.axis_index("group"), lax.axis_index("mp")
    mp_bits = bits_of("mp")
    length = SEQ // n_mp
    half = D // 2

    up = lax.all_to_all(gen_up, "dp", split_axis=1, concat_axis=0, tiled=True)
    gen_down, up = lax.optimization_barrier((gen_down, up))
    down = lax.all_to_all(gen_down, "dp", split_axis=0, concat_axis=1, tiled=True)
    share = up.shape[1]
    up = xor_gather(up, "mp", mp_bits).reshape(n_mp, half, share)
    up = up.transpose(1, 0, 2).reshape(half, n_mp * share)
    up = jnp.concatenate([up, swap(up, "group", 1)], axis=0)
    down = xor_gather(down, "mp", mp_bits).reshape(n_mp * share, half)
    down_other = swap(down, "group", 1)
    down = jnp.where(
        group == 0,
        jnp.concatenate([down, down_other], axis=1),
        jnp.concatenate([down_other, down], axis=1),
    )

    seeds = lax.all_gather(noise_seeds, "dp", tiled=True)[:, None, None]
    shape = (n_dp, length, D)
    tokens = lax.broadcasted_iota(jnp.int32, shape, 1) + mp * length
    feature = (lax.broadcasted_iota(jnp.int32, shape, 2) + group * half) % D
    normed = rms_norm(hashed(seeds, 0, tokens, feature)).astype(jnp.bfloat16)
    normed = normed.reshape(n_dp * length, D)
    before = jnp.dot(normed, up, preferred_element_type=jnp.float32)
    hidden = jax.nn.gelu(before, approximate=True).astype(jnp.bfloat16)

    parts = jnp.dot(hidden, down, preferred_element_type=jnp.float32).astype(jnp.bfloat16)
    mixed = sum_over_dp(parts.reshape(n_dp, length, D))

    own_seed = noise_seeds[:, None]
    tokens = lax.broadcasted_iota(jnp.int32, (length, D), 0) + mp * length
    feature = lax.broadcasted_iota(jnp.int32, (length, D), 1)
    latent = (hashed(own_seed, 0, tokens, feature) + mixed).astype(jnp.bfloat16)
    shift = (timestep_ids.astype(jnp.float32) + 0.5) / STEPS
    fresh = hashed(own_seed, 1, tokens, feature)
    noisy = ((1.0 - shift) * latent.astype(jnp.float32) + shift * fresh).astype(jnp.bfloat16)
    score_normed = rms_norm(noisy.astype(jnp.float32)).astype(jnp.bfloat16)

    sample = xor_gather(score_normed, "mp", mp_bits).reshape(SEQ, D)
    paired = jnp.stack([sample, swap(sample, "group", 1)])
    latents = tokens_to_features(latent, "mp")
    other_pred, own_pred = score_forward(paired, score_qkv[0], score_out[0])
    partner = swap(other_pred.astype(jnp.bfloat16), "group", 1)
    flip_sign = (2 * group - 1).astype(jnp.float32)
    gap = flip_sign * (own_pred - partner.astype(jnp.float32))
    gap = xor_scatter(gap.reshape((2,) * len(mp_bits) + (length, D)), "mp", mp_bits)
    gap = gap.astype(jnp.bfloat16)
    gap, latents = lax.optimization_barrier((gap, latents))
    gap_all = gather_over_dp(gap).reshape(n_dp * length, D)
    score_gap = tokens_to_features(gap, "mp")

    def over_batch(value):
        return value / batch_size

    down_sent = over_batch(
        contract_first(hidden, lax.dynamic_slice_in_dim(gap_all, (1 - group) * half, half, 1))
    ).astype(jnp.bfloat16)
    gap_all, down_sent = lax.optimization_barrier((gap_all, down_sent))
    down_sent = swap(down_sent, "group", 1)
    down_kept = over_batch(
        contract_first(hidden, lax.dynamic_slice_in_dim(gap_all, group * half, half, 1))
    )
    gap_all, down_kept = lax.optimization_barrier((gap_all, down_kept))
    grad_down = (down_kept + down_sent.astype(jnp.float32)).astype(jnp.bfloat16)
    grad_down = grad_down.reshape((2,) * len(mp_bits) + (share, half))
    grad_down = xor_scatter(grad_down, "mp", mp_bits).astype(jnp.bfloat16)
    grad_down = lax.all_to_all(grad_down, "dp", split_axis=1, concat_axis=0, tiled=True)

    slope = lax.dot_general(
        gap_all, down, (((1,), (1,)), ((), ())), preferred_element_type=jnp.float32
    )
    change = (slope * gelu_slope(before)).astype(jnp.bfloat16)
    change, score_gap = lax.optimization_barrier((change, score_gap))
    up_sent = over_batch(contract_first(normed[:, half:], change)).astype(jnp.bfloat16)
    up_sent = swap(up_sent, "group", 1)
    up_kept = over_batch(contract_first(normed[:, :half], change))
    grad_up = (up_kept + up_sent.astype(jnp.float32)).astype(jnp.bfloat16)
    grad_up = jnp.moveaxis(grad_up.reshape(half, n_mp, share), 1, 0)
    grad_up = grad_up.reshape((2,) * len(mp_bits) + (half, share))
    grad_up = xor_scatter(grad_up, "mp", mp_bits).astype(jnp.bfloat16)
    grad_up = lax.all_to_all(grad_up, "dp", split_axis=0, concat_axis=1, tiled=True)
    return (latents[None], score_gap[None], grad_up, grad_down)


def solution(mesh):
    in_specs = (
        P(("group", "dp")),
        P(("group", "dp")),
        P(("group", "dp"), "mp"),
        P("mp", ("group", "dp")),
        P("group", None, None, "mp"),
        P("group", "mp", None),
    )
    out_specs = (
        P(("group", "dp"), None, "mp"),
        P(("group", "dp"), None, "mp"),
        P(("group", "dp"), "mp"),
        P("mp", ("group", "dp")),
    )
    return jax.shard_map(
        per_device, mesh=mesh, in_specs=in_specs, out_specs=out_specs, check_vma=False
    )
```

```python
import functools

import jax
import jax.numpy as jnp
from jax import lax
from jax.experimental import pallas as pl
from jax.experimental.pallas import tpu as pltpu
from jax.sharding import PartitionSpec as P

D = 3072
HEAD_DIM = 128
SEQ = 256
STEPS = 1000


NORM_EPS = 1e-06
ROOT_THREE = 1.7320508
GELU_SCALE = 0.7978845608


def swap(shard, axis, bit):
    return lax.ppermute(shard, axis, [(i, i ^ bit) for i in range(lax.axis_size(axis))])


def bits_of(axis):
    return [1 << k for k in range(lax.axis_size(axis).bit_length() - 1)]


def xor_gather(shard, axis, order):
    bits = bits_of(axis)
    out = shard.reshape((1,) * len(bits) + shard.shape)
    for bit in order:
        out = jnp.concatenate([out, swap(out, axis, bit)], axis=bits.index(bit))
    return out


def xor_scatter(parts, axis, order, beside=None):
    bits = bits_of(axis)
    for bit in order:
        at = bits.index(bit)
        kept = lax.slice_in_dim(parts, 0, 1, axis=at)
        sent = lax.slice_in_dim(parts, 1, 2, axis=at).astype(jnp.bfloat16)
        came = swap(sent, axis, bit)
        if beside is not None and bit == order[0]:
            came, beside = lax.optimization_barrier((came, beside))
        parts = kept.astype(jnp.float32) + came.astype(jnp.float32)
    parts = parts.reshape(parts.shape[len(bits):])
    return parts if beside is None else (parts, beside)


def tokens_to_features(shard, axis):
    count = lax.axis_size(axis)
    me = lax.axis_index(axis)
    tokens, width = shard.shape[0], shard.shape[1] // count
    out = jnp.zeros((count * tokens, width), shard.dtype)
    for mask in range(count):
        other = me ^ mask
        block = lax.dynamic_slice_in_dim(shard, other * width, width, 1)
        if mask:
            block = swap(block, axis, mask)
        out = lax.dynamic_update_slice_in_dim(out, block, other * tokens, 0)
    return out


def hashed(seed_grid, stream, tokens, feature):
    mixing = seed_grid * 747796405 + stream * 374761393 + tokens * 1103515245 + feature * 668265263
    mixing = mixing ^ mixing >> 15
    mixing = mixing * 1274126177
    mixing = mixing ^ mixing >> 13
    mixing = mixing * 1911520717
    mixing = mixing ^ mixing >> 16
    level = (mixing >> 7 & 65535).astype(jnp.float32)
    return ((level + 0.5) * (2.0 / 65536.0) - 1.0) * ROOT_THREE


ROWS = 16


def greet(spot, line, pair):
    barrier = pltpu.get_barrier_semaphore()

    def signal(to):
        pl.semaphore_signal(
            barrier, inc=1, device_id={"dp": to}, device_id_type=pl.DeviceIdType.MESH
        )

    me = lax.axis_index("dp")
    signal(pair)

    @pl.when(spot > 0)
    def _():
        signal(me - 2)

    @pl.when(spot < line - 1)
    def _():
        signal(me + 2)

    ends = (spot == 0).astype(jnp.int32) + (spot == line - 1).astype(jnp.int32)
    pl.semaphore_wait(barrier, 3 - ends)


def remote(source, target, send_sem, recv_sem, to):
    return pltpu.make_async_remote_copy(
        src_ref=source,
        dst_ref=target,
        send_sem=send_sem,
        recv_sem=recv_sem,
        device_id={"dp": to},
        device_id_type=pl.DeviceIdType.MESH,
    )


def sum_kernel(line, parts, out, paired, lower, upper, p_send, p_recv, l_send, l_recv, u_send, u_recv):
    me = lax.axis_index("dp")
    side, spot = lax.rem(me, 2), lax.div(me, 2)
    pair = me + 1 - 2 * side
    steps = parts.shape[1] // ROWS
    greet(spot, line, pair)

    def to_pair(d):
        return remote(parts.at[2 * d + 1 - side], paired.at[d], p_send.at[d], p_recv.at[d], pair)

    def to_next(d):
        return remote(paired.at[d], lower.at[d], l_send.at[d], l_recv.at[d], me + 2)

    def to_last(d):
        return remote(paired.at[d], upper.at[d], u_send.at[d], u_recv.at[d], me - 2)

    def add(target, d, terms):
        @pl.loop(0, steps)
        def _(step):
            rows = pl.ds(pl.multiple_of(step * ROWS, ROWS), ROWS)
            total = parts[2 * d + side, rows].astype(jnp.float32)
            for term in terms:
                total = total + term[d, rows].astype(jnp.float32)
            if target is out:
                out[rows] = total
            else:
                target[d, rows] = total.astype(jnp.bfloat16)

    for far in range(line - 1, 0, -1):

        @pl.when(spot + far < line)
        def _():
            to_pair(spot + far).start()

        @pl.when(spot - far >= 0)
        def _():
            to_pair(spot - far).start()

    to_pair(spot).start()

    for far in range(line - 1, 0, -1):
        up, down = spot + far, spot - far

        @pl.when(up < line)
        def _():
            to_pair(up).wait_recv()

            @pl.when(spot > 0)
            def _():
                to_next(up).wait_recv()
                add(paired, up, (paired, lower))

            @pl.when(spot == 0)
            def _():
                add(paired, up, (paired,))

            to_next(up).start()

        @pl.when(down >= 0)
        def _():
            to_pair(down).wait_recv()

            @pl.when(spot < line - 1)
            def _():
                to_last(down).wait_recv()
                add(paired, down, (paired, upper))

            @pl.when(spot == line - 1)
            def _():
                add(paired, down, (paired,))

            to_last(down).start()

    to_pair(spot).wait_recv()

    @pl.when(spot == 0)
    def _():
        to_last(spot).wait_recv()
        add(out, spot, (paired, upper))

    @pl.when(spot == line - 1)
    def _():
        to_next(spot).wait_recv()
        add(out, spot, (paired, lower))

    @pl.when((spot > 0) & (spot < line - 1))
    def _():
        to_next(spot).wait_recv()
        to_last(spot).wait_recv()
        add(out, spot, (paired, lower, upper))

    for d in range(line):
        to_pair(d).wait_send()

        @pl.when(d > spot)
        def _():
            to_next(d).wait_send()

        @pl.when(d < spot)
        def _():
            to_last(d).wait_send()


def sum_over_dp(parts):
    line = parts.shape[0] // 2
    block = parts.shape[1:]
    slots = pltpu.VMEM((line,) + block, jnp.bfloat16)
    return pl.pallas_call(
        functools.partial(sum_kernel, line),
        out_shape=jax.ShapeDtypeStruct(block, jnp.float32),
        in_specs=[pl.BlockSpec(memory_space=pltpu.VMEM)],
        out_specs=pl.BlockSpec(memory_space=pltpu.VMEM),
        scratch_shapes=[slots] * 3 + [pltpu.SemaphoreType.DMA((line,))] * 6,
        compiler_params=pltpu.CompilerParams(
            collective_id=0, has_side_effects=True, vmem_limit_bytes=40 << 20
        ),
        cost_estimate=pl.CostEstimate(
            flops=2 * parts.size, bytes_accessed=40 * parts.size, transcendentals=0
        ),
    )(parts)


def gather_kernel(line, own, out, own_sem, recv, p_send, n_send, l_send):
    me = lax.axis_index("dp")
    side, spot = lax.rem(me, 2), lax.div(me, 2)
    pair = me + 1 - 2 * side
    greet(spot, line, pair)

    def source(d, first):
        return own if first else out.at[2 * d + side]

    def move(d, sems, to, first=False):
        b = 2 * d + side
        return remote(source(d, first), out.at[b], sems.at[d], recv.at[b], to)

    def arrived(b):
        remote(out.at[b], out.at[b], p_send.at[0], recv.at[b], pair).wait_recv()

    kept = pltpu.make_async_copy(own, out.at[me], own_sem)

    @pl.when(spot < line - 1)
    def _():
        move(spot, n_send, me + 2, True).start()

    @pl.when(spot > 0)
    def _():
        move(spot, l_send, me - 2, True).start()

    move(spot, p_send, pair, True).start()
    kept.start()
    for far in range(1, line):
        low, high = spot - far, spot + far

        @pl.when(low >= 0)
        def _():
            arrived(2 * low + side)

            @pl.when(spot < line - 1)
            def _():
                move(low, n_send, me + 2).start()

            move(low, p_send, pair).start()

        @pl.when(high < line)
        def _():
            arrived(2 * high + side)

            @pl.when(spot > 0)
            def _():
                move(high, l_send, me - 2).start()

            move(high, p_send, pair).start()

    for d in range(line):
        arrived(2 * d + 1 - side)
        move(d, p_send, pair).wait_send()

        @pl.when((d <= spot) & (spot < line - 1))
        def _():
            move(d, n_send, me + 2).wait_send()

        @pl.when((d >= spot) & (spot > 0))
        def _():
            move(d, l_send, me - 2).wait_send()

    kept.wait()


def gather_over_dp(own):
    count = lax.axis_size("dp")
    line = count // 2
    return pl.pallas_call(
        functools.partial(gather_kernel, line),
        out_shape=jax.ShapeDtypeStruct((count,) + own.shape, own.dtype),
        in_specs=[pl.BlockSpec(memory_space=pl.ANY)],
        out_specs=pl.BlockSpec(memory_space=pl.ANY),
        scratch_shapes=[
            pltpu.SemaphoreType.DMA(()),
            pltpu.SemaphoreType.DMA((count,)),
            pltpu.SemaphoreType.DMA((line,)),
            pltpu.SemaphoreType.DMA((line,)),
            pltpu.SemaphoreType.DMA((line,)),
        ],
        compiler_params=pltpu.CompilerParams(collective_id=1, has_side_effects=True),
        cost_estimate=pl.CostEstimate(
            flops=0, bytes_accessed=40 * count * own.size, transcendentals=0
        ),
    )(own)


def rms_norm(value):
    return value * lax.rsqrt(jnp.mean(value * value, axis=-1, keepdims=True) + NORM_EPS)


def gelu_slope(value):
    inner = GELU_SCALE * (value + 0.044715 * value * value * value)
    bend = jnp.tanh(inner)
    return 0.5 * (1.0 + bend) + 0.5 * value * (1.0 - bend * bend) * GELU_SCALE * (
        1.0 + 3.0 * 0.044715 * value * value
    )


def project(normed, weights_in):
    return jnp.einsum(
        "bsd,kdh->kbsh", normed, weights_in, preferred_element_type=jnp.float32
    ).astype(jnp.bfloat16)


def attend(projected):
    pairs, length, width = projected[0].shape
    local_heads = width // HEAD_DIM
    shape = (pairs, length, local_heads, HEAD_DIM)
    query = projected[0].reshape(shape)
    keys = projected[1].reshape(shape)
    values = projected[2].reshape(shape)
    scores = jnp.einsum(
        "bqhe,bkhe->bhqk", query, keys, preferred_element_type=jnp.float32
    ) * HEAD_DIM ** (-0.5)
    expo = jnp.exp(scores)
    probs = (expo / jnp.sum(expo, axis=-1, keepdims=True)).astype(jnp.bfloat16)
    attended = jnp.einsum(
        "bhqk,bkhe->bqhe", probs, values, preferred_element_type=jnp.float32
    ).astype(jnp.bfloat16)
    return attended.reshape(pairs, length, width)


def contract_first(left, right):
    return lax.dot_general(left, right, (((0,), (0,)), ((), ())), preferred_element_type=jnp.float32)


def per_device(noise_seeds, timestep_ids, gen_up, gen_down, score_qkv, score_out):
    n_dp, n_mp = lax.axis_size("dp"), lax.axis_size("mp")
    batch_size = lax.axis_size("group") * n_dp
    group, mp = lax.axis_index("group"), lax.axis_index("mp")
    mp_bits = bits_of("mp")
    length = SEQ // n_mp
    half = D // 2

    up = lax.all_to_all(gen_up, "dp", split_axis=1, concat_axis=0, tiled=True)
    gen_down, up = lax.optimization_barrier((gen_down, up))
    down = lax.all_to_all(gen_down, "dp", split_axis=0, concat_axis=1, tiled=True)
    share = up.shape[1]
    up = xor_gather(up, "mp", mp_bits).reshape(n_mp, half, share)
    up = up.transpose(1, 0, 2).reshape(half, n_mp * share)
    up = jnp.concatenate([up, swap(up, "group", 1)], axis=0)
    down = xor_gather(down, "mp", mp_bits).reshape(n_mp * share, half)
    down_other = swap(down, "group", 1)
    down = jnp.where(
        group == 0,
        jnp.concatenate([down, down_other], axis=1),
        jnp.concatenate([down_other, down], axis=1),
    )

    seeds = xor_gather(noise_seeds, "dp", bits_of("dp")[::-1])
    seeds = seeds.transpose(tuple(range(seeds.ndim))[::-1]).reshape(1, n_dp)
    index = lax.broadcasted_iota(jnp.int32, (n_dp, n_dp), 0)
    column = lax.broadcasted_iota(jnp.int32, (n_dp, n_dp), 1)
    seeds = jnp.sum(jnp.where(index ^ lax.axis_index("dp") == column, seeds, 0), axis=1)
    seeds = seeds[:, None, None]
    shape = (n_dp, length, D)
    tokens = lax.broadcasted_iota(jnp.int32, shape, 1) + mp * length
    feature = (lax.broadcasted_iota(jnp.int32, shape, 2) + group * half) % D
    normed = rms_norm(hashed(seeds, 0, tokens, feature)).astype(jnp.bfloat16)
    normed = normed.reshape(n_dp * length, D)
    before = jnp.dot(normed, up, preferred_element_type=jnp.float32)
    hidden = jax.nn.gelu(before, approximate=True).astype(jnp.bfloat16)

    parts = jnp.dot(hidden, down, preferred_element_type=jnp.float32).astype(jnp.bfloat16)
    mixed = sum_over_dp(parts.reshape(n_dp, length, D))

    own_seed = noise_seeds[:, None]
    tokens = lax.broadcasted_iota(jnp.int32, (length, D), 0) + mp * length
    feature = lax.broadcasted_iota(jnp.int32, (length, D), 1)
    latent = (hashed(own_seed, 0, tokens, feature) + mixed).astype(jnp.bfloat16)
    shift = (timestep_ids.astype(jnp.float32) + 0.5) / STEPS
    fresh = hashed(own_seed, 1, tokens, feature)
    noisy = ((1.0 - shift) * latent.astype(jnp.float32) + shift * fresh).astype(jnp.bfloat16)
    score_normed = rms_norm(noisy.astype(jnp.float32)).astype(jnp.bfloat16)

    sample = xor_gather(score_normed, "mp", mp_bits).reshape(SEQ, D)
    near = jnp.stack([score_normed, swap(score_normed, "group", 1)])
    near = project(near, score_qkv[0])
    sample, near = lax.optimization_barrier((sample[length:], near))
    far = project(jnp.stack([sample, swap(sample, "group", 1)]), score_qkv[0])
    latents = tokens_to_features(latent, "mp")
    attended = attend([jnp.concatenate([near[k], far[k]], axis=1) for k in range(3)])

    def predict(pair, start, stop):
        return jnp.dot(
            attended[pair, start:stop], score_out[0], preferred_element_type=jnp.float32
        )

    flip_sign = (2 * group - 1).astype(jnp.float32)
    split = SEQ // 2
    sent = [
        predict(1, start, start + split).astype(jnp.bfloat16) for start in (split, 0)
    ]
    came = [swap(part, "group", 1) for part in sent]
    gap = [
        flip_sign * (predict(0, start, start + split) - part.astype(jnp.float32))
        for start, part in zip((split, 0), came)
    ]
    gap = [part.astype(jnp.bfloat16) for part in gap]
    blocks = (1,) + (2,) * (len(mp_bits) - 1) + (length, D)
    came = swap(gap[0].reshape(blocks), "mp", mp_bits[0])
    gap = gap[1].reshape(blocks).astype(jnp.float32) + came.astype(jnp.float32)
    for at, bit in enumerate(mp_bits[1:], 1):
        kept = lax.slice_in_dim(gap, 0, 1, axis=at)
        came = swap(lax.slice_in_dim(gap, 1, 2, axis=at).astype(jnp.bfloat16), "mp", bit)
        gap = kept + came.astype(jnp.float32)
    gap = gap.reshape(length, D).astype(jnp.bfloat16)
    gap, latents = lax.optimization_barrier((gap, latents))
    gap_all = gather_over_dp(gap).reshape(n_dp * length, D)
    score_gap = tokens_to_features(gap, "mp")

    def over_batch(value):
        return value / batch_size

    down_sent = over_batch(
        contract_first(hidden, lax.dynamic_slice_in_dim(gap_all, (1 - group) * half, half, 1))
    ).astype(jnp.bfloat16)
    gap_all, down_sent = lax.optimization_barrier((gap_all, down_sent))
    down_sent = swap(down_sent, "group", 1)
    down_kept = over_batch(
        contract_first(hidden, lax.dynamic_slice_in_dim(gap_all, group * half, half, 1))
    )
    gap_all, down_kept = lax.optimization_barrier((gap_all, down_kept))
    grad_down = (down_kept + down_sent.astype(jnp.float32)).astype(jnp.bfloat16)
    grad_down = grad_down.reshape((2,) * len(mp_bits) + (share, half))

    slope = lax.dot_general(
        gap_all, down, (((1,), (1,)), ((), ())), preferred_element_type=jnp.float32
    )
    change = (slope * gelu_slope(before)).astype(jnp.bfloat16)
    change, score_gap, grad_down = lax.optimization_barrier((change, score_gap, grad_down))
    up_sent = over_batch(contract_first(normed[:, half:], change)).astype(jnp.bfloat16)
    up_sent = swap(up_sent, "group", 1)
    up_kept = over_batch(contract_first(normed[:, :half], change))
    grad_up = (up_kept + up_sent.astype(jnp.float32)).astype(jnp.bfloat16)
    grad_up = jnp.moveaxis(grad_up.reshape(half, n_mp, share), 1, 0)
    grad_up = grad_up.reshape((2,) * len(mp_bits) + (half, share))
    grad_down, grad_up = xor_scatter(grad_down, "mp", mp_bits, grad_up)
    grad_down = grad_down.astype(jnp.bfloat16)
    grad_down = lax.all_to_all(grad_down, "dp", split_axis=1, concat_axis=0, tiled=True)
    grad_up = xor_scatter(grad_up, "mp", mp_bits).astype(jnp.bfloat16)
    grad_up = lax.all_to_all(grad_up, "dp", split_axis=0, concat_axis=1, tiled=True)
    return (latents[None], score_gap[None], grad_up, grad_down)


def solution(mesh):
    in_specs = (
        P(("group", "dp")),
        P(("group", "dp")),
        P(("group", "dp"), "mp"),
        P("mp", ("group", "dp")),
        P("group", None, None, "mp"),
        P("group", "mp", None),
    )
    out_specs = (
        P(("group", "dp"), None, "mp"),
        P(("group", "dp"), None, "mp"),
        P(("group", "dp"), "mp"),
        P("mp", ("group", "dp")),
    )
    return jax.shard_map(
        per_device, mesh=mesh, in_specs=in_specs, out_specs=out_specs, check_vma=False
    )
```

```python
import functools

import jax
import jax.numpy as jnp
from jax import lax
from jax.experimental import pallas as pl
from jax.experimental.pallas import tpu as pltpu
from jax.sharding import PartitionSpec as P

D = 3072
HEAD_DIM = 128
SEQ = 256
STEPS = 1000


NORM_EPS = 1e-06
ROOT_THREE = 1.7320508
GELU_SCALE = 0.7978845608


def swap(shard, axis, bit):
    return lax.ppermute(shard, axis, [(i, i ^ bit) for i in range(lax.axis_size(axis))])


def bits_of(axis):
    return [1 << k for k in range(lax.axis_size(axis).bit_length() - 1)]


def xor_gather(shard, axis, order):
    bits = bits_of(axis)
    out = shard.reshape((1,) * len(bits) + shard.shape)
    for bit in order:
        out = jnp.concatenate([out, swap(out, axis, bit)], axis=bits.index(bit))
    return out


def xor_scatter(parts, axis, order, beside=None):
    bits = bits_of(axis)
    for bit in order:
        at = bits.index(bit)
        kept = lax.slice_in_dim(parts, 0, 1, axis=at)
        sent = lax.slice_in_dim(parts, 1, 2, axis=at).astype(jnp.bfloat16)
        came = swap(sent, axis, bit)
        if beside is not None and bit == order[0]:
            came, beside = lax.optimization_barrier((came, beside))
        parts = kept.astype(jnp.float32) + came.astype(jnp.float32)
    parts = parts.reshape(parts.shape[len(bits):])
    return parts if beside is None else (parts, beside)


def tokens_to_features(shard, axis):
    count = lax.axis_size(axis)
    me = lax.axis_index(axis)
    tokens, width = shard.shape[0], shard.shape[1] // count
    out = jnp.zeros((count * tokens, width), shard.dtype)
    for mask in range(count):
        other = me ^ mask
        block = lax.dynamic_slice_in_dim(shard, other * width, width, 1)
        if mask:
            block = swap(block, axis, mask)
        out = lax.dynamic_update_slice_in_dim(out, block, other * tokens, 0)
    return out


def hashed(seed_grid, stream, tokens, feature):
    mixing = seed_grid * 747796405 + stream * 374761393 + tokens * 1103515245 + feature * 668265263
    mixing = mixing ^ mixing >> 15
    mixing = mixing * 1274126177
    mixing = mixing ^ mixing >> 13
    mixing = mixing * 1911520717
    mixing = mixing ^ mixing >> 16
    level = (mixing >> 7 & 65535).astype(jnp.float32)
    return ((level + 0.5) * (2.0 / 65536.0) - 1.0) * ROOT_THREE


ROWS = 16


def greet(spot, line, pair):
    barrier = pltpu.get_barrier_semaphore()

    def signal(to):
        pl.semaphore_signal(
            barrier, inc=1, device_id={"dp": to}, device_id_type=pl.DeviceIdType.MESH
        )

    me = lax.axis_index("dp")
    signal(pair)

    @pl.when(spot > 0)
    def _():
        signal(me - 2)

    @pl.when(spot < line - 1)
    def _():
        signal(me + 2)

    ends = (spot == 0).astype(jnp.int32) + (spot == line - 1).astype(jnp.int32)
    pl.semaphore_wait(barrier, 3 - ends)


def remote(source, target, send_sem, recv_sem, to):
    return pltpu.make_async_remote_copy(
        src_ref=source,
        dst_ref=target,
        send_sem=send_sem,
        recv_sem=recv_sem,
        device_id={"dp": to},
        device_id_type=pl.DeviceIdType.MESH,
    )


def sum_kernel(line, parts, out, paired, lower, upper, p_send, p_recv, l_send, l_recv, u_send, u_recv):
    me = lax.axis_index("dp")
    side, spot = lax.rem(me, 2), lax.div(me, 2)
    pair = me + 1 - 2 * side
    steps = parts.shape[1] // ROWS
    greet(spot, line, pair)

    def to_pair(d):
        return remote(parts.at[2 * d + 1 - side], paired.at[d], p_send.at[d], p_recv.at[d], pair)

    def to_next(d):
        return remote(paired.at[d], lower.at[d], l_send.at[d], l_recv.at[d], me + 2)

    def to_last(d):
        return remote(paired.at[d], upper.at[d], u_send.at[d], u_recv.at[d], me - 2)

    def add(target, d, terms):
        @pl.loop(0, steps)
        def _(step):
            rows = pl.ds(pl.multiple_of(step * ROWS, ROWS), ROWS)
            total = parts[2 * d + side, rows].astype(jnp.float32)
            for term in terms:
                total = total + term[d, rows].astype(jnp.float32)
            if target is out:
                out[rows] = total
            else:
                target[d, rows] = total.astype(jnp.bfloat16)

    for far in range(line - 1, 0, -1):

        @pl.when(spot + far < line)
        def _():
            to_pair(spot + far).start()

        @pl.when(spot - far >= 0)
        def _():
            to_pair(spot - far).start()

    to_pair(spot).start()

    for far in range(line - 1, 0, -1):
        up, down = spot + far, spot - far

        @pl.when(up < line)
        def _():
            to_pair(up).wait_recv()

            @pl.when(spot > 0)
            def _():
                to_next(up).wait_recv()
                add(paired, up, (paired, lower))

            @pl.when(spot == 0)
            def _():
                add(paired, up, (paired,))

            to_next(up).start()

        @pl.when(down >= 0)
        def _():
            to_pair(down).wait_recv()

            @pl.when(spot < line - 1)
            def _():
                to_last(down).wait_recv()
                add(paired, down, (paired, upper))

            @pl.when(spot == line - 1)
            def _():
                add(paired, down, (paired,))

            to_last(down).start()

    to_pair(spot).wait_recv()

    @pl.when(spot == 0)
    def _():
        to_last(spot).wait_recv()
        add(out, spot, (paired, upper))

    @pl.when(spot == line - 1)
    def _():
        to_next(spot).wait_recv()
        add(out, spot, (paired, lower))

    @pl.when((spot > 0) & (spot < line - 1))
    def _():
        to_next(spot).wait_recv()
        to_last(spot).wait_recv()
        add(out, spot, (paired, lower, upper))

    for d in range(line):
        to_pair(d).wait_send()

        @pl.when(d > spot)
        def _():
            to_next(d).wait_send()

        @pl.when(d < spot)
        def _():
            to_last(d).wait_send()


def sum_over_dp(parts):
    line = parts.shape[0] // 2
    block = parts.shape[1:]
    slots = pltpu.VMEM((line,) + block, jnp.bfloat16)
    return pl.pallas_call(
        functools.partial(sum_kernel, line),
        out_shape=jax.ShapeDtypeStruct(block, jnp.float32),
        in_specs=[pl.BlockSpec(memory_space=pltpu.VMEM)],
        out_specs=pl.BlockSpec(memory_space=pltpu.VMEM),
        scratch_shapes=[slots] * 3 + [pltpu.SemaphoreType.DMA((line,))] * 6,
        compiler_params=pltpu.CompilerParams(
            collective_id=0, has_side_effects=True, vmem_limit_bytes=40 << 20
        ),
        cost_estimate=pl.CostEstimate(
            flops=2 * parts.size, bytes_accessed=40 * parts.size, transcendentals=0
        ),
    )(parts)


def gather_kernel(line, own, out, own_sem, recv, p_send, n_send, l_send):
    me = lax.axis_index("dp")
    side, spot = lax.rem(me, 2), lax.div(me, 2)
    pair = me + 1 - 2 * side
    greet(spot, line, pair)

    def source(d, first):
        return own if first else out.at[2 * d + side]

    def move(d, sems, to, first=False):
        b = 2 * d + side
        return remote(source(d, first), out.at[b], sems.at[d], recv.at[b], to)

    def arrived(b):
        remote(out.at[b], out.at[b], p_send.at[0], recv.at[b], pair).wait_recv()

    kept = pltpu.make_async_copy(own, out.at[me], own_sem)

    @pl.when(spot < line - 1)
    def _():
        move(spot, n_send, me + 2, True).start()

    @pl.when(spot > 0)
    def _():
        move(spot, l_send, me - 2, True).start()

    move(spot, p_send, pair, True).start()
    kept.start()
    for far in range(1, line):
        low, high = spot - far, spot + far

        @pl.when(low >= 0)
        def _():
            arrived(2 * low + side)

            @pl.when(spot < line - 1)
            def _():
                move(low, n_send, me + 2).start()

            move(low, p_send, pair).start()

        @pl.when(high < line)
        def _():
            arrived(2 * high + side)

            @pl.when(spot > 0)
            def _():
                move(high, l_send, me - 2).start()

            move(high, p_send, pair).start()

    for d in range(line):
        arrived(2 * d + 1 - side)
        move(d, p_send, pair).wait_send()

        @pl.when((d <= spot) & (spot < line - 1))
        def _():
            move(d, n_send, me + 2).wait_send()

        @pl.when((d >= spot) & (spot > 0))
        def _():
            move(d, l_send, me - 2).wait_send()

    kept.wait()


def gather_over_dp(own):
    count = lax.axis_size("dp")
    line = count // 2
    return pl.pallas_call(
        functools.partial(gather_kernel, line),
        out_shape=jax.ShapeDtypeStruct((count,) + own.shape, own.dtype),
        in_specs=[pl.BlockSpec(memory_space=pl.ANY)],
        out_specs=pl.BlockSpec(memory_space=pl.ANY),
        scratch_shapes=[
            pltpu.SemaphoreType.DMA(()),
            pltpu.SemaphoreType.DMA((count,)),
            pltpu.SemaphoreType.DMA((line,)),
            pltpu.SemaphoreType.DMA((line,)),
            pltpu.SemaphoreType.DMA((line,)),
        ],
        compiler_params=pltpu.CompilerParams(collective_id=1, has_side_effects=True),
        cost_estimate=pl.CostEstimate(
            flops=0, bytes_accessed=40 * count * own.size, transcendentals=0
        ),
    )(own)


def rms_norm(value):
    return value * lax.rsqrt(jnp.mean(value * value, axis=-1, keepdims=True) + NORM_EPS)


def gelu_slope(value):
    inner = GELU_SCALE * (value + 0.044715 * value * value * value)
    bend = jnp.tanh(inner)
    return 0.5 * (1.0 + bend) + 0.5 * value * (1.0 - bend * bend) * GELU_SCALE * (
        1.0 + 3.0 * 0.044715 * value * value
    )


def project(normed, weights_in):
    return jnp.einsum(
        "bsd,kdh->kbsh", normed, weights_in, preferred_element_type=jnp.float32
    ).astype(jnp.bfloat16)


def attend(projected):
    pairs, length, width = projected[0].shape
    local_heads = width // HEAD_DIM
    shape = (pairs, length, local_heads, HEAD_DIM)
    query = projected[0].reshape(shape)
    keys = projected[1].reshape(shape)
    values = projected[2].reshape(shape)
    scores = jnp.einsum(
        "bqhe,bkhe->bhqk", query, keys, preferred_element_type=jnp.float32
    ) * HEAD_DIM ** (-0.5)
    expo = jnp.exp(scores)
    probs = (expo / jnp.sum(expo, axis=-1, keepdims=True)).astype(jnp.bfloat16)
    attended = jnp.einsum(
        "bhqk,bkhe->bqhe", probs, values, preferred_element_type=jnp.float32
    ).astype(jnp.bfloat16)
    return attended.reshape(pairs, length, width)


def contract_first(left, right):
    return lax.dot_general(left, right, (((0,), (0,)), ((), ())), preferred_element_type=jnp.float32)


def per_device(noise_seeds, timestep_ids, gen_up, gen_down, score_qkv, score_out):
    n_dp, n_mp = lax.axis_size("dp"), lax.axis_size("mp")
    batch_size = lax.axis_size("group") * n_dp
    group, mp = lax.axis_index("group"), lax.axis_index("mp")
    mp_bits = bits_of("mp")
    length = SEQ // n_mp
    half = D // 2

    seeds = [noise_seeds] + [swap(noise_seeds, "dp", mask) for mask in range(1, n_dp)]
    seeds = jnp.concatenate(seeds)[None]
    index = lax.broadcasted_iota(jnp.int32, (n_dp, n_dp), 0)
    column = lax.broadcasted_iota(jnp.int32, (n_dp, n_dp), 1)
    seeds = jnp.sum(jnp.where(index ^ lax.axis_index("dp") == column, seeds, 0), axis=1)
    seeds = seeds[:, None, None]
    shape = (n_dp, length, D)
    tokens = lax.broadcasted_iota(jnp.int32, shape, 1) + mp * length
    feature = (lax.broadcasted_iota(jnp.int32, shape, 2) + group * half) % D
    normed = rms_norm(hashed(seeds, 0, tokens, feature)).astype(jnp.bfloat16)
    normed = normed.reshape(n_dp * length, D)
    up = lax.all_to_all(gen_up, "dp", split_axis=1, concat_axis=0, tiled=True)
    gen_down, up, normed = lax.optimization_barrier((gen_down, up, normed))
    down = lax.all_to_all(gen_down, "dp", split_axis=0, concat_axis=1, tiled=True)
    share = up.shape[1]
    up, down = lax.optimization_barrier((xor_gather(up, "mp", mp_bits), down))
    up = up.reshape(n_mp, half, share)
    up = up.transpose(1, 0, 2).reshape(half, n_mp * share)
    up = jnp.concatenate([up, swap(up, "group", 1)], axis=0)
    down = xor_gather(down, "mp", mp_bits).reshape(n_mp * share, half)
    down_other = swap(down, "group", 1)
    down = jnp.where(
        group == 0,
        jnp.concatenate([down, down_other], axis=1),
        jnp.concatenate([down_other, down], axis=1),
    )

    before = jnp.dot(normed, up, preferred_element_type=jnp.float32)
    hidden = jax.nn.gelu(before, approximate=True).astype(jnp.bfloat16)

    parts = jnp.dot(hidden, down, preferred_element_type=jnp.float32).astype(jnp.bfloat16)
    mixed = sum_over_dp(parts.reshape(n_dp, length, D))

    own_seed = noise_seeds[:, None]
    tokens = lax.broadcasted_iota(jnp.int32, (length, D), 0) + mp * length
    feature = lax.broadcasted_iota(jnp.int32, (length, D), 1)
    latent = (hashed(own_seed, 0, tokens, feature) + mixed).astype(jnp.bfloat16)
    shift = (timestep_ids.astype(jnp.float32) + 0.5) / STEPS
    fresh = hashed(own_seed, 1, tokens, feature)
    noisy = ((1.0 - shift) * latent.astype(jnp.float32) + shift * fresh).astype(jnp.bfloat16)
    score_normed = rms_norm(noisy.astype(jnp.float32)).astype(jnp.bfloat16)

    sample = xor_gather(score_normed, "mp", mp_bits).reshape(SEQ, D)
    near = jnp.stack([score_normed, swap(score_normed, "group", 1)])
    near = project(near, score_qkv[0])
    sample, near = lax.optimization_barrier((sample[length:], near))
    far = project(jnp.stack([sample, swap(sample, "group", 1)]), score_qkv[0])
    latents = tokens_to_features(latent, "mp")
    attended = attend([jnp.concatenate([near[k], far[k]], axis=1) for k in range(3)])

    def predict(pair, start, stop):
        return jnp.dot(
            attended[pair, start:stop], score_out[0], preferred_element_type=jnp.float32
        )

    flip_sign = (2 * group - 1).astype(jnp.float32)
    split = SEQ // 2
    sent = [
        predict(1, start, start + split).astype(jnp.bfloat16) for start in (split, 0)
    ]
    came = [swap(part, "group", 1) for part in sent]
    gap = [
        flip_sign * (predict(0, start, start + split) - part.astype(jnp.float32))
        for start, part in zip((split, 0), came)
    ]
    gap = [part.astype(jnp.bfloat16) for part in gap]
    blocks = (1,) + (2,) * (len(mp_bits) - 1) + (length, D)
    came = swap(gap[0].reshape(blocks), "mp", mp_bits[0])
    gap = gap[1].reshape(blocks).astype(jnp.float32) + came.astype(jnp.float32)
    for at, bit in enumerate(mp_bits[1:], 1):
        kept = lax.slice_in_dim(gap, 0, 1, axis=at)
        came = swap(lax.slice_in_dim(gap, 1, 2, axis=at).astype(jnp.bfloat16), "mp", bit)
        gap = kept + came.astype(jnp.float32)
    gap = gap.reshape(length, D).astype(jnp.bfloat16)
    gap, latents = lax.optimization_barrier((gap, latents))
    gap_all = gather_over_dp(gap).reshape(n_dp * length, D)

    def over_batch(value):
        return value / batch_size

    down_sent = over_batch(
        contract_first(hidden, lax.dynamic_slice_in_dim(gap_all, (1 - group) * half, half, 1))
    ).astype(jnp.bfloat16)
    gap_all, down_sent = lax.optimization_barrier((gap_all, down_sent))
    down_sent = swap(down_sent, "group", 1)
    down_kept = over_batch(
        contract_first(hidden, lax.dynamic_slice_in_dim(gap_all, group * half, half, 1))
    )
    gap_all, down_kept = lax.optimization_barrier((gap_all, down_kept))
    grad_down = (down_kept + down_sent.astype(jnp.float32)).astype(jnp.bfloat16)
    grad_down = grad_down.reshape((2,) * len(mp_bits) + (share, half))
    gap_all, grad_down = lax.optimization_barrier((gap_all, grad_down))

    slope = lax.dot_general(
        gap_all, down, (((1,), (1,)), ((), ())), preferred_element_type=jnp.float32
    )
    change = (slope * gelu_slope(before)).astype(jnp.bfloat16)
    up_sent = over_batch(contract_first(normed[:, half:], change)).astype(jnp.bfloat16)
    up_sent = swap(up_sent, "group", 1)
    up_kept = over_batch(contract_first(normed[:, :half], change))
    grad_up = (up_kept + up_sent.astype(jnp.float32)).astype(jnp.bfloat16)
    grad_up = jnp.moveaxis(grad_up.reshape(half, n_mp, share), 1, 0)
    grad_up = grad_up.reshape((2,) * len(mp_bits) + (half, share))
    grad_down, grad_up = xor_scatter(grad_down, "mp", mp_bits, grad_up)
    grad_down = grad_down.astype(jnp.bfloat16)
    grad_down = lax.all_to_all(grad_down, "dp", split_axis=1, concat_axis=0, tiled=True)
    grad_up = xor_scatter(grad_up, "mp", mp_bits).astype(jnp.bfloat16)
    grad_up, gap = lax.optimization_barrier((grad_up, gap))
    score_gap = tokens_to_features(gap, "mp")
    grad_up = lax.all_to_all(grad_up, "dp", split_axis=0, concat_axis=1, tiled=True)
    return (latents[None], score_gap[None], grad_up, grad_down)


def solution(mesh):
    in_specs = (
        P(("group", "dp")),
        P(("group", "dp")),
        P(("group", "dp"), "mp"),
        P("mp", ("group", "dp")),
        P("group", None, None, "mp"),
        P("group", "mp", None),
    )
    out_specs = (
        P(("group", "dp"), None, "mp"),
        P(("group", "dp"), None, "mp"),
        P(("group", "dp"), "mp"),
        P("mp", ("group", "dp")),
    )
    return jax.shard_map(
        per_device, mesh=mesh, in_specs=in_specs, out_specs=out_specs, check_vma=False
    )
```
